32 devices in a mesh: seq: 8 (over z, core), tensor: 4 (over y, x).
Axes of the slice: x: 2, y: 2, z: 4, core: 2. Of those that a mesh axis runs over, the one named last changes fastest.
Arguments:
- tokens: bfloat16 [1024, 8192], P('seq', 'tensor'), may hold values from -2000 to 2000
- cotangent: bfloat16 [1024, 8192], P('seq', 'tensor'), may hold values from -6 to 6
- gain: float32 [8192], P('tensor'), may hold values from 0.25 to 1.75
- w_gate: bfloat16 [8192, 14336], P('tensor', 'seq'), may hold values from -0.0625 to 0.0625
- w_up: bfloat16 [8192, 14336], P('tensor', 'seq'), may hold values from -0.0625 to 0.0625
- w_down: bfloat16 [14336, 8192], P('seq', 'tensor'), may hold values from -0.046875 to 0.046875
- probe: bfloat16 [8192, 14336], P('tensor', 'seq'), may hold values from -1 to 1, as said below
Outputs:
- hessian_probe: float32 [8192, 14336], P('tensor', 'seq')
The draws below stay inside these ranges and needn't reach their ends.
Inputs may be any that keep to these rules, and one draw needn't show every extreme that they name: `probe`: every entry is +1 or -1.
All inputs are finite; a program needn't handle non-finite values.
Results may differ from the reference program's by a relative error of at most 0.024.
Values may be sent and summed in bfloat16 or wider, within the bound.
A program may use at most 128 MiB of HBM per device.

```python
import math
import jax
import jax.numpy as jnp
from jax import lax

D = 8192
FF = 14336
TOKENS = 1024
N_TENSOR = 4


def draw_tokens(key, part):
    base_key, row_key, column_key = jax.random.split(key, 3)
    position = jnp.arange(D, dtype=jnp.float32) / (D - 1)
    column_rough = jnp.exp(jax.random.uniform(column_key, (1, D), jnp.float32, 0.0, math.log(3.0)))
    random_part = jax.random.normal(base_key, (TOKENS, D), jnp.float32)
    row_scale = jnp.exp(jax.random.uniform(row_key, (TOKENS, 1), jnp.float32, 0.0, math.log(10.0)))
    column_trend = jnp.exp(position * math.log(4.0))[None, :]
    values = random_part * row_scale * column_trend * column_rough
    return jnp.clip(values, -2000.0, 2000.0).astype(jnp.bfloat16)


def draw_probe(key, part):
    coin_flips = jax.random.randint(key, (D, FF), 0, 2)
    return (2.0 * coin_flips.astype(jnp.float32) - 1.0).astype(jnp.bfloat16)


def shard_levels(own_key, shape, cuts, low, largest):
    def one(dim, shards_of):
        steps = jax.random.uniform(jax.random.fold_in(jax.random.fold_in(own_key, 6), dim), (shards_of,), jnp.float32, low / len(cuts), largest / len(cuts))
        return jnp.repeat(jnp.exp(steps), shape[dim] // shards_of).reshape((-1,) + (1,) * (len(shape) - dim - 1))

    factor_of = one(*cuts[0])
    for cut in cuts[1:]:
        factor_of = factor_of * one(*cut)
    return factor_of


def centred(rng, shape, scale, limit, cuts=(), kind=jnp.bfloat16):
    entries = jax.random.normal(rng, shape, jnp.float32) * scale
    if len(cuts) > 0:
        entries = shard_levels(rng, shape, cuts, -0.22, 0.18) * entries
    return jnp.clip(entries, min=-limit, max=limit).astype(kind)


def setup_inputs(seed: int = 0) -> dict:
    seeds = jax.random.split(jax.random.key(seed), 8)
    return {
        "tokens": draw_tokens(jax.random.fold_in(seeds[7], 71), 0),
        "cotangent": centred(seeds[1], (TOKENS, D), 1.0, 6.0, ((0, 8), (1, 4))),
        "gain": jnp.clip(1.0 + 0.15 * jax.random.normal(seeds[2], (D,), jnp.float32), 0.25, 1.75),
        "w_gate": centred(seeds[3], (D, FF), D ** -0.5, 0.0625, ((0, 4), (1, 8))),
        "w_up": centred(seeds[4], (D, FF), D ** -0.5, 0.0625, ((0, 4), (1, 8))),
        "w_down": centred(seeds[5], (FF, D), FF ** -0.5, 0.046875, ((0, 8), (1, 4))),
        "probe": draw_probe(jax.random.fold_in(seeds[7], 71), 0),
    }


epsilon = 1e-05

def blocked_product(left, right, contract_right):
    block_width = D // N_TENSOR

    def advance(running, block_index):
        offset = block_index * block_width
        left_block = lax.dynamic_slice_in_dim(left, offset, block_width, 1)
        right_block = lax.dynamic_slice_in_dim(right, offset, block_width, contract_right)
        partial_sum = lax.dot_general(left_block, right_block, (((1,), (contract_right,)), ((), ())), preferred_element_type=jnp.float32)
        rounded = lax.optimization_barrier(partial_sum.astype(jnp.bfloat16))
        return (running + rounded.astype(jnp.float32), None)
    output_width = right.shape[1 - contract_right]
    start_value = jnp.zeros((left.shape[0], output_width), jnp.float32)
    result, _ = lax.scan(advance, start_value, jnp.arange(N_TENSOR, dtype=jnp.int32))
    return result

def second_factor(pre_gate, pre_up, tangent, upstream):
    sigmoid_gate = jax.nn.sigmoid(pre_gate)
    curvature = sigmoid_gate * (1.0 - sigmoid_gate) * (2.0 + pre_gate * (1.0 - 2.0 * sigmoid_gate))
    return (upstream * pre_up * curvature * tangent).astype(jnp.bfloat16)

def reference(tokens, cotangent, gain, w_gate, w_up, w_down, probe):
    values = tokens.astype(jnp.float32)
    inverse = lax.rsqrt(lax.optimization_barrier(jnp.sum(values * values, axis=1)) / D + epsilon)
    normed = (values * inverse[:, None] * gain[None, :]).astype(jnp.bfloat16)
    pre_gate = blocked_product(normed, w_gate, 0)
    pre_up = blocked_product(normed, w_up, 0)
    tangent = blocked_product(normed, probe, 0)
    upstream = blocked_product(cotangent, w_down, 1)
    second = second_factor(pre_gate, pre_up, tangent, upstream)
    product = lax.dot_general(normed, second, (((0,), (0,)), ((), ())), preferred_element_type=jnp.float32)
    return product / TOKENS
```

```python
import functools

import jax
import jax.numpy as jnp
from jax import lax
from jax.sharding import PartitionSpec as P

epsilon = 1e-05


def second_factor(pre_gate, pre_up, tangent, upstream):
    sigmoid_gate = jax.nn.sigmoid(pre_gate)
    curvature = sigmoid_gate * (1.0 - sigmoid_gate) * (2.0 + pre_gate * (1.0 - 2.0 * sigmoid_gate))
    return (upstream * pre_up * curvature * tangent).astype(jnp.bfloat16)


def swap(value, axis, size, mask):
    return lax.ppermute(value, axis, [(i, i ^ mask) for i in range(size)])


def bit_of(bit):
    return (lax.axis_index("tensor") >> bit) & 1


def scatter_sum(parts, order, size):
    bits = len(order)
    rows, width = parts[0].shape
    left = list(range(bits - 1, -1, -1))
    held = [part.reshape([2] * bits + [rows // size, width]) for part in parts]
    for bit in order:
        place = left.index(bit)
        mine = bit_of(bit)
        sent = jnp.concatenate(
            [lax.dynamic_index_in_dim(h, 1 - mine, place, False).astype(jnp.bfloat16) for h in held], axis=-1
        )
        came = swap(sent, "tensor", size, 1 << bit)
        held = [
            lax.dynamic_index_in_dim(h, mine, place, False).astype(jnp.float32)
            + came[..., k * width : (k + 1) * width].astype(jnp.float32)
            for k, h in enumerate(held)
        ]
        left.pop(place)
    return held


def gather_rows(block, order, size):
    done = []
    for bit in order:
        place = sum(1 for other in done if other > bit)
        mine = bit_of(bit)
        came = swap(block, "tensor", size, 1 << bit)
        low = jnp.where(mine == 0, block, came)
        high = jnp.where(mine == 0, came, block)
        block = jnp.stack([low, high], axis=place)
        done.append(bit)
    return block.reshape(-1, block.shape[-1])


def arrival(chip, step, chips):
    both = min(chip, chips - 1 - chip)
    if step <= 2 * both:
        return ("left" if step % 2 else "right", (step + 1) // 2)
    return ("left" if chip > chips - 1 - chip else "right", step - both)


def body(n_seq, n_tensor, tokens, cotangent, gain, w_gate, w_up, w_down, probe):
    chips = n_seq // 2
    bits = n_tensor.bit_length() - 1
    up_order = list(range(bits))
    down_order = up_order[::-1]
    rows = tokens.shape[0]
    features = tokens.shape[1] * n_tensor
    total_tokens = rows * n_seq

    values = tokens.astype(jnp.float32)
    squares = jnp.sum(values * values, axis=1)
    for bit in up_order:
        squares = squares + swap(squares, "tensor", n_tensor, 1 << bit)
    inverse = lax.rsqrt(squares / features + epsilon)
    normed = (values * inverse[:, None] * gain[None, :]).astype(jnp.bfloat16)

    own = jnp.concatenate([normed, cotangent], axis=0)
    rightward = [(i, i + 2) for i in range(n_seq - 2)]
    leftward = [(i + 2, i) for i in range(n_seq - 2)]
    came = {("left", 0): own, ("right", 0): own}
    for distance in range(1, chips):
        came["left", distance] = lax.ppermute(came["left", distance - 1], "seq", rightward)
        came["right", distance] = lax.ppermute(came["right", distance - 1], "seq", leftward)
    chip = lax.axis_index("seq") // 2

    chunks = []
    for step in range(chips):
        if step == 0:
            norm_rows = jnp.concatenate([normed, swap(normed, "seq", n_seq, 1)], axis=0)
            cot_rows = jnp.concatenate([cotangent, swap(cotangent, "seq", n_seq, 1)], axis=0)
        else:
            where_from = [arrival(c, step, chips) for c in range(chips)]
            block = came[where_from[0]]
            for c in range(1, chips):
                if where_from[c] != where_from[0]:
                    block = jnp.where(chip == c, came[where_from[c]], block)
            other = swap(block, "seq", n_seq, 1)
            norm_rows = jnp.concatenate([block[:rows], other[:rows]], axis=0)
            cot_rows = jnp.concatenate([block[rows:], other[rows:]], axis=0)

        upstream = lax.dot_general(
            cot_rows, w_down, (((1,), (1,)), ((), ())), preferred_element_type=jnp.float32
        ).astype(jnp.bfloat16)
        tangent, pre_gate, pre_up = [
            jnp.dot(norm_rows, weight, preferred_element_type=jnp.float32).astype(jnp.bfloat16)
            for weight in (probe, w_gate, w_up)
        ]
        upstream, tangent = scatter_sum([upstream, tangent], up_order, n_tensor)
        pre_gate, pre_up = scatter_sum([pre_gate, pre_up], down_order, n_tensor)
        second = second_factor(pre_gate, pre_up, tangent, upstream)
        half = second.shape[1] // 2
        second = jnp.concatenate(
            [
                gather_rows(second[:, :half], up_order, n_tensor),
                gather_rows(second[:, half:], down_order, n_tensor),
            ],
            axis=1,
        )
        chunks.append((norm_rows, second))

    def product(some):
        return lax.dot_general(
            jnp.concatenate([c[0] for c in some], axis=0),
            jnp.concatenate([c[1] for c in some], axis=0),
            (((0,), (0,)), ((), ())),
            preferred_element_type=jnp.float32,
        )

    early = product(chunks[:-1])
    return (early + product(chunks[-1:])) / total_tokens


def solution(mesh):
    return jax.shard_map(
        functools.partial(body, mesh.shape["seq"], mesh.shape["tensor"]),
        mesh=mesh,
        in_specs=(
            P("seq", "tensor"),
            P("seq", "tensor"),
            P("tensor"),
            P("tensor", "seq"),
            P("tensor", "seq"),
            P("seq", "tensor"),
            P("tensor", "seq"),
        ),
        out_specs=P("tensor", "seq"),
        check_vma=False,
    )
```

```python
import functools

import jax
import jax.numpy as jnp
from jax import lax
from jax.experimental import pallas as pl
from jax.experimental.pallas import tpu as pltpu
from jax.sharding import PartitionSpec as P

epsilon = 1e-05


def second_factor(pre_gate, pre_up, tangent, upstream):
    sigmoid_gate = jax.nn.sigmoid(pre_gate)
    curvature = sigmoid_gate * (1.0 - sigmoid_gate) * (2.0 + pre_gate * (1.0 - 2.0 * sigmoid_gate))
    return (upstream * pre_up * curvature * tangent).astype(jnp.bfloat16)


def swap(value, axis, size, mask):
    return lax.ppermute(value, axis, [(i, i ^ mask) for i in range(size)])


def bit_of(bit):
    return (lax.axis_index("tensor") >> bit) & 1


def after(value, waited):
    return lax.optimization_barrier((value, waited))[0]


def scatter_sum(parts, order, size):
    bits = len(order)
    rows, width = parts[0].shape
    left = list(range(bits - 1, -1, -1))
    held = [part.reshape([2] * bits + [rows // size, width]) for part in parts]
    first = None
    for bit in order:
        place = left.index(bit)
        mine = bit_of(bit)
        sent = [lax.dynamic_index_in_dim(h, 1 - mine, place, False).astype(jnp.bfloat16) for h in held]
        if first is None:
            came = [swap(one, "tensor", size, 1 << bit) for one in sent]
        else:
            came = swap(jnp.concatenate(sent, axis=-1), "tensor", size, 1 << bit)
            came = [came[..., k * width : (k + 1) * width] for k in range(len(held))]
        first = came[0] if first is None else first
        held = [
            lax.dynamic_index_in_dim(h, mine, place, False).astype(jnp.float32)
            + c.astype(jnp.float32)
            for h, c in zip(held, came)
        ]
        left.pop(place)
    return held, first


def gather_rows(block, order, size):
    done = []
    for bit in order:
        place = sum(1 for other in done if other > bit)
        mine = bit_of(bit)
        came = swap(block, "tensor", size, 1 << bit)
        low = jnp.where(mine == 0, block, came)
        high = jnp.where(mine == 0, came, block)
        block = jnp.stack([low, high], axis=place)
        done.append(bit)
    return block.reshape(-1, block.shape[-1])


def arrival(chip, step, chips):
    both = min(chip, chips - 1 - chip)
    if step <= 2 * both:
        return ("left" if step % 2 else "right", (step + 1) // 2)
    return ("left" if chip > chips - 1 - chip else "right", step - both)


def product_kernel(scale, left_ref, right_ref, out_ref):
    out_ref[...] = jnp.dot(left_ref[...], right_ref[...], preferred_element_type=jnp.float32) * scale


def scaled_product(left, right, scale):
    rows, depth = left.shape
    width = right.shape[1]
    tile = 256
    return pl.pallas_call(
        functools.partial(product_kernel, scale),
        grid=(rows // tile,),
        in_specs=[
            pl.BlockSpec((tile, depth), lambda i: (i, 0)),
            pl.BlockSpec((depth, width), lambda i: (0, 0)),
        ],
        out_specs=pl.BlockSpec((tile, width), lambda i: (i, 0)),
        out_shape=jax.ShapeDtypeStruct((rows, width), jnp.float32),
        compiler_params=pltpu.CompilerParams(vmem_limit_bytes=32 * 1024 * 1024),
        cost_estimate=pl.CostEstimate(
            flops=2 * rows * depth * width,
            bytes_accessed=2 * depth * (rows + width) + 4 * rows * width,
            transcendentals=0,
        ),
    )(left, right)


def rows_kernel(transposed, left_ref, *refs):
    weights, outs = refs[: len(refs) // 2], refs[len(refs) // 2 :]
    for weight_ref, out_ref in zip(weights, outs):
        out_ref[...] = lax.dot_general(
            left_ref[...],
            weight_ref[...],
            (((1,), (1 if transposed else 0,)), ((), ())),
            preferred_element_type=jnp.float32,
        ).astype(out_ref.dtype)


def rows_products(left, weights, transposed):
    rows, depth = left.shape
    width = weights[0].shape[0 if transposed else 1]
    tile = 256 if width % 256 == 0 else 128
    if transposed:
        weight_spec = pl.BlockSpec((tile, depth), lambda i: (i, 0))
    else:
        weight_spec = pl.BlockSpec((depth, tile), lambda i: (0, i))
    count = len(weights)
    return pl.pallas_call(
        functools.partial(rows_kernel, transposed),
        grid=(width // tile,),
        in_specs=[pl.BlockSpec((rows, depth), lambda i: (0, 0))] + [weight_spec] * count,
        out_specs=[pl.BlockSpec((rows, tile), lambda i: (0, i))] * count,
        out_shape=[jax.ShapeDtypeStruct((rows, width), jnp.bfloat16)] * count,
        compiler_params=pltpu.CompilerParams(vmem_limit_bytes=24 * 1024 * 1024),
        cost_estimate=pl.CostEstimate(
            flops=2 * count * rows * depth * width,
            bytes_accessed=2 * (rows * depth + count * width * (rows + depth)),
            transcendentals=0,
        ),
    )(left, *weights)


def body(n_seq, n_tensor, tokens, cotangent, gain, w_gate, w_up, w_down, probe):
    chips = n_seq // 2
    bits = n_tensor.bit_length() - 1
    up_order = list(range(bits))
    down_order = up_order[::-1]
    rows = tokens.shape[0]
    features = tokens.shape[1] * n_tensor
    total_tokens = rows * n_seq

    values = tokens.astype(jnp.float32)
    squares = jnp.sum(values * values, axis=1)
    for bit in up_order:
        squares = squares + swap(squares, "tensor", n_tensor, 1 << bit)
    inverse = lax.rsqrt(squares / features + epsilon)
    normed = (values * inverse[:, None] * gain[None, :]).astype(jnp.bfloat16)

    own = jnp.concatenate([normed, cotangent], axis=0)
    rightward = [(i, i + 2) for i in range(n_seq - 2)]
    leftward = [(i + 2, i) for i in range(n_seq - 2)]
    came = {("left", 0): own, ("right", 0): own}

    def pass_on(distance, waited):
        left, right = after((came["left", distance - 1], came["right", distance - 1]), waited)
        came["left", distance] = lax.ppermute(left, "seq", rightward)
        came["right", distance] = lax.ppermute(right, "seq", leftward)

    pass_on(1, ())
    chip = lax.axis_index("seq") // 2

    def products(norm_rows, cot_rows):
        return [
            *rows_products(cot_rows, [w_down], True),
            *rows_products(norm_rows, [probe, w_gate, w_up], False),
        ]

    def gathered(one, other):
        return [gather_rows(one, up_order, n_tensor), gather_rows(other, down_order, n_tensor)]

    def gathered_alone(second):
        half = second.shape[1] // 2
        return jnp.concatenate(gathered(second[:, :half], second[:, half:]), axis=1)

    all_norm, all_second, firsts, seconds = [], [], [], []
    for step in range(chips):
        if step == 0:
            cot_rows = jnp.concatenate([cotangent, swap(cotangent, "seq", n_seq, 1)], axis=0)
            norm_rows = jnp.concatenate([normed, swap(normed, "seq", n_seq, 1)], axis=0)
        else:
            where_from = [arrival(c, step, chips) for c in range(chips)]
            kinds = sorted(set(where_from))
            candidates = after([came[kind] for kind in kinds], (firsts[step - 1], seconds[: step - 1]))
            block = candidates[0]
            for kind, candidate in zip(kinds[1:], candidates[1:]):
                for c in range(chips):
                    if where_from[c] == kind:
                        block = jnp.where(chip == c, candidate, block)
            other = swap(block, "seq", n_seq, 1)
            norm_rows = jnp.concatenate([block[:rows], other[:rows]], axis=0)
            cot_rows = jnp.concatenate([block[rows:], other[rows:]], axis=0)
        all_norm.append(norm_rows)
        if step == chips - 1:
            norm_columns = jnp.concatenate(all_norm, axis=0).T
            cot_rows, norm_columns = lax.optimization_barrier((cot_rows, norm_columns))

        parts = products(norm_rows, cot_rows)
        if step == chips - 1:
            ready = after(seconds, parts)
            while len(ready) > 1:
                all_second += gathered(ready[0], ready[1])
                ready = ready[2:]
            all_second += [gathered_alone(one) for one in ready]
        upstream, tangent, pre_gate, pre_up = parts
        (upstream, pre_gate), first = scatter_sum([upstream, pre_gate], up_order, n_tensor)
        (tangent, pre_up), other_first = scatter_sum([tangent, pre_up], down_order, n_tensor)
        firsts.append((first, other_first))
        if step < chips - 2:
            pass_on(step + 2, (firsts[-1], seconds))
        second = second_factor(pre_gate, pre_up, tangent, upstream)
        seconds.append(second)

    all_second.append(gathered_alone(seconds[-1]))
    return scaled_product(norm_columns, jnp.concatenate(all_second, axis=0), 1.0 / total_tokens)


def solution(mesh):
    return jax.shard_map(
        functools.partial(body, mesh.shape["seq"], mesh.shape["tensor"]),
        mesh=mesh,
        in_specs=(
            P("seq", "tensor"),
            P("seq", "tensor"),
            P("tensor"),
            P("tensor", "seq"),
            P("tensor", "seq"),
            P("seq", "tensor"),
            P("tensor", "seq"),
        ),
        out_specs=P("tensor", "seq"),
        check_vma=False,
    )
```

```python
import functools

import jax
import jax.numpy as jnp
from jax import lax
from jax.experimental import pallas as pl
from jax.experimental.pallas import tpu as pltpu
from jax.sharding import PartitionSpec as P

epsilon = 1e-05


def second_factor(pre_gate, pre_up, tangent, upstream):
    sigmoid_gate = jax.nn.sigmoid(pre_gate)
    curvature = sigmoid_gate * (1.0 - sigmoid_gate) * (2.0 + pre_gate * (1.0 - 2.0 * sigmoid_gate))
    return (upstream * pre_up * curvature * tangent).astype(jnp.bfloat16)


def swap(value, axis, size, mask):
    return lax.ppermute(value, axis, [(i, i ^ mask) for i in range(size)])


def bit_of(bit):
    return (lax.axis_index("tensor") >> bit) & 1


def after(value, waited):
    return lax.optimization_barrier((value, waited))[0]


def scatter_sum(parts, order, size):
    bits = len(order)
    rows, width = parts[0].shape
    left = list(range(bits - 1, -1, -1))
    held = [part.reshape([2] * bits + [rows // size, width]) for part in parts]
    first = None
    for bit in order:
        place = left.index(bit)
        mine = bit_of(bit)
        sent = [lax.dynamic_index_in_dim(h, 1 - mine, place, False).astype(jnp.bfloat16) for h in held]
        if first is None:
            came = [swap(one, "tensor", size, 1 << bit) for one in sent]
        else:
            came = swap(jnp.concatenate(sent, axis=-1), "tensor", size, 1 << bit)
            came = [came[..., k * width : (k + 1) * width] for k in range(len(held))]
        first = came[0] if first is None else first
        held = [lax.dynamic_index_in_dim(h, mine, place, False) for h in held]
        left.pop(place)
        if left:
            held = add(held, came)
    return held, came, first


def add(held, came):
    return [h.astype(jnp.float32) + c.astype(jnp.float32) for h, c in zip(held, came)]


def gather_rows(block, order, size):
    done = []
    for bit in order:
        place = sum(1 for other in done if other > bit)
        mine = bit_of(bit)
        came = swap(block, "tensor", size, 1 << bit)
        low = jnp.where(mine == 0, block, came)
        high = jnp.where(mine == 0, came, block)
        block = jnp.stack([low, high], axis=place)
        done.append(bit)
    return block.reshape(-1, block.shape[-1])


def arrival(chip, step, chips):
    both = min(chip, chips - 1 - chip)
    if step <= 2 * both:
        return ("left" if step % 2 else "right", (step + 1) // 2)
    return ("left" if chip > chips - 1 - chip else "right", step - both)


def product_kernel(scale, places, n_left, *refs):
    lefts, rights, out_ref, right = refs[:n_left], refs[n_left:-2], refs[-2], refs[-1]

    @pl.when(pl.program_id(0) == 0)
    def _():
        for (row, column), ref in zip(places, rights):
            right[row : row + ref.shape[0], column : column + ref.shape[1]] = ref[...]

    left = jnp.concatenate([ref[...] for ref in lefts], axis=0)
    out_ref[...] = scale * lax.dot_general(
        left, right[...], (((0,), (0,)), ((), ())), preferred_element_type=jnp.float32
    )


def scaled_product(lefts, left_rows, rights, places, scale):
    depth = left_rows * len(lefts)
    rows = lefts[0].shape[1]
    width = max(column + right.shape[1] for (_, column), right in zip(places, rights))
    tile = 256
    return pl.pallas_call(
        functools.partial(product_kernel, scale, places, len(lefts)),
        grid=(rows // tile,),
        in_specs=[pl.BlockSpec((left_rows, tile), lambda i: (0, i))] * len(lefts)
        + [pl.BlockSpec(right.shape, lambda i: (0, 0)) for right in rights],
        out_specs=pl.BlockSpec((tile, width), lambda i: (i, 0)),
        out_shape=jax.ShapeDtypeStruct((rows, width), jnp.float32),
        scratch_shapes=[pltpu.VMEM((depth, width), jnp.bfloat16)],
        compiler_params=pltpu.CompilerParams(vmem_limit_bytes=60 * 1024 * 1024),
        cost_estimate=pl.CostEstimate(
            flops=2 * rows * depth * width,
            bytes_accessed=2 * depth * (rows + width) + 4 * rows * width,
            transcendentals=0,
        ),
    )(*lefts, *rights)


def rows_kernel(transposed, upper_ref, lower_ref, *refs):
    weights, outs = refs[: len(refs) // 2], refs[len(refs) // 2 :]
    left = jnp.concatenate([upper_ref[...], lower_ref[...]], axis=0)
    for weight_ref, out_ref in zip(weights, outs):
        out_ref[...] = lax.dot_general(
            left,
            weight_ref[...],
            (((1,), (1 if transposed else 0,)), ((), ())),
            preferred_element_type=jnp.float32,
        ).astype(out_ref.dtype)


def rows_products(upper, lower, part, half_rows, weights, transposed):
    rows, depth = 2 * half_rows, upper.shape[1]
    width = weights[0].shape[0 if transposed else 1]
    tile = 256 if width % 256 == 0 else 128
    if transposed:
        weight_spec = pl.BlockSpec((tile, depth), lambda i: (i, 0))
    else:
        weight_spec = pl.BlockSpec((depth, tile), lambda i: (0, i))
    count = len(weights)
    return pl.pallas_call(
        functools.partial(rows_kernel, transposed),
        grid=(width // tile,),
        in_specs=[pl.BlockSpec((half_rows, depth), lambda i: (part, 0))] * 2 + [weight_spec] * count,
        out_specs=[pl.BlockSpec((rows, tile), lambda i: (0, i))] * count,
        out_shape=[jax.ShapeDtypeStruct((rows, width), jnp.bfloat16)] * count,
        compiler_params=pltpu.CompilerParams(vmem_limit_bytes=60 * 1024 * 1024),
        cost_estimate=pl.CostEstimate(
            flops=2 * count * rows * depth * width,
            bytes_accessed=2 * (rows * depth + count * width * (rows + depth)),
            transcendentals=0,
        ),
    )(upper, lower, *weights)


def body(n_seq, n_tensor, tokens, cotangent, gain, w_gate, w_up, w_down, probe):
    chips = n_seq // 2
    bits = n_tensor.bit_length() - 1
    up_order = list(range(bits))
    down_order = up_order[::-1]
    rows = tokens.shape[0]
    features = tokens.shape[1] * n_tensor
    total_tokens = rows * n_seq

    values = tokens.astype(jnp.float32)
    squares = jnp.sum(values * values, axis=1)
    for bit in up_order:
        squares = squares + swap(squares, "tensor", n_tensor, 1 << bit)
    inverse = lax.rsqrt(squares / features + epsilon)
    normed = (values * inverse[:, None] * gain[None, :]).astype(jnp.bfloat16)

    own = jnp.concatenate([normed, cotangent], axis=0)
    rightward = [(i, i + 2) for i in range(n_seq - 2)]
    leftward = [(i + 2, i) for i in range(n_seq - 2)]
    came = {("left", 0): own, ("right", 0): own}

    def pass_on(distance, waited):
        left, right = after((came["left", distance - 1], came["right", distance - 1]), waited)
        came["left", distance] = lax.ppermute(left, "seq", rightward)
        came["right", distance] = lax.ppermute(right, "seq", leftward)

    pass_on(1, ())
    chip = lax.axis_index("seq") // 2

    def gathered(one, other):
        return [gather_rows(one, up_order, n_tensor), gather_rows(other, down_order, n_tensor)]

    all_norm, rights, places, firsts, seconds = [], [], [], [], []
    unfinished = None

    def finished(waited):
        held, came = unfinished
        upstream, pre_gate, tangent, pre_up = add(held, after(came, waited))
        return second_factor(pre_gate, pre_up, tangent, upstream)

    def gather_last(step, second):
        half = second.shape[1] // 2
        rights.extend(gathered(second[:, :half], second[:, half:]))
        places.extend([(2 * rows * step, 0), (2 * rows * step, half)])

    for step in range(chips):
        if step == 0:
            cots = (cotangent, swap(cotangent, "seq", n_seq, 1), 0)
            norms = (normed, swap(normed, "seq", n_seq, 1), 0)
        else:
            where_from = [arrival(c, step, chips) for c in range(chips)]
            kinds = sorted(set(where_from))
            candidates = after([came[kind] for kind in kinds], (firsts[step - 1], seconds))
            block = candidates[0]
            for kind, candidate in zip(kinds[1:], candidates[1:]):
                for c in range(chips):
                    if where_from[c] == kind:
                        block = jnp.where(chip == c, candidate, block)
            other = swap(block, "seq", n_seq, 1)
            cots = (block, other, 1)
            norms = (block, other, 0)
        all_norm += norms[:2]

        parts = [
            *rows_products(*cots, rows, [w_down], True),
            *rows_products(*norms, rows, [probe, w_gate, w_up], False),
        ]
        if step > 0:
            seconds.append(finished(parts))
        if step == chips - 1:
            ready = list(enumerate(after(seconds, parts)))
            while len(ready) > 1:
                rights += gathered(ready[0][1], ready[1][1])
                places += [(2 * rows * ready[0][0], 0), (2 * rows * ready[1][0], 0)]
                ready = ready[2:]
            for index, second in ready:
                gather_last(index, second)
        upstream, tangent, pre_gate, pre_up = parts
        held, last, first = scatter_sum([upstream, pre_gate], up_order, n_tensor)
        other_held, other_last, other_first = scatter_sum([tangent, pre_up], down_order, n_tensor)
        unfinished = (held + other_held, last + other_last)
        firsts.append((first, other_first))
        if step < chips - 2:
            pass_on(step + 2, (firsts[-1], seconds))

    gather_last(chips - 1, finished(()))
    return scaled_product(all_norm, rows, rights, places, 1.0 / total_tokens)


def solution(mesh):
    return jax.shard_map(
        functools.partial(body, mesh.shape["seq"], mesh.shape["tensor"]),
        mesh=mesh,
        in_specs=(
            P("seq", "tensor"),
            P("seq", "tensor"),
            P("tensor"),
            P("tensor", "seq"),
            P("tensor", "seq"),
            P("seq", "tensor"),
            P("tensor", "seq"),
        ),
        out_specs=P("tensor", "seq"),
        check_vma=False,
    )
```
